1024 devices in a mesh: node: 8 (over x, core), local: 32 (over z), dp: 4 (over y).
Axes of the slice: x: 4, y: 4, z: 32, core: 2. Of those that a mesh axis runs over, the one named last changes fastest.
Arguments:
- grad_out: bfloat16 [24576, 3584], P(('node', 'local', 'dp')), may hold values from -6 to 6
- expert_ids: int32 [24576, 8], P(('node', 'local', 'dp')), may hold values from 0 to 255, as said below
- slot_ids: int32 [24576, 8], P(('node', 'local', 'dp')), may hold values from -1 to 5, as said below
- gate_values: bfloat16 [24576, 8], P(('node', 'local', 'dp')), may hold values from 0.049804688 to 0.59765625
- hidden: bfloat16 [256, 768, 1024], P(('node', 'local'), 'dp'), may hold values from -0.59765625 to 0.59765625
Outputs:
- grad_weight: bfloat16 [256, 3584, 1024], P(('node', 'local'), 'dp')
The draws below stay inside these ranges and needn't reach their ends.
Inputs may be any that keep to these rules, and one draw needn't show every extreme that they name: `expert_ids`: each row names 8 different experts, which lie in at most 4 groups; expert e belongs to group e // 32. For one expert and the tokens of all devices that share a local index and a dp index, the assignments with slot_ids >= 0 have different slots; -1 marks a dropped assignment. In every dp replica some expert has all 6 slots filled for every local index.
All inputs are finite; a program needn't handle non-finite values.
Results may differ from the reference program's by a relative error of at most 0.013.
Values may be sent and summed in bfloat16 or wider, within the bound.
A program may use at most 32 MiB of HBM per device.

```python
import jax
import jax.numpy as jnp
from jax import lax

D = 3584
FF = 1024
TOPK = 8
GROUPS_TOK = 4
TOK_DEV = 24
EXPERTS = 256
CAP_BLOCK = 6
CAPACITY = 192
TOKENS = 24576
N_NODE = 8
N_LOCAL = 32
N_DP = 4


def routing(key):
    split_keys = jax.random.split(key, 5)
    block_tokens = N_NODE * TOK_DEV
    forced_count = min(CAP_BLOCK + 2, block_tokens)
    tokens = jnp.arange(TOKENS, dtype=jnp.int32)
    replica = tokens // TOK_DEV % N_DP
    favourite = jax.random.randint(split_keys[0], (N_DP,), 0, EXPERTS)
    hot_expert = favourite[replica]
    random_draws = jax.random.randint(split_keys[1], (N_LOCAL, N_DP, block_tokens), 0, 2 ** 20)
    distinct = random_draws * block_tokens + jnp.arange(block_tokens, dtype=jnp.int32)
    order_rank = jnp.argsort(jnp.argsort(distinct, axis=-1), axis=-1)
    forced = (order_rank < forced_count).reshape(N_LOCAL, N_DP, N_NODE, TOK_DEV)
    forced = jnp.transpose(forced, (2, 0, 1, 3)).reshape(TOKENS)
    node_ids = jnp.arange(N_NODE, dtype=jnp.int32)
    group_score = jax.random.randint(split_keys[2], (TOKENS, N_NODE), 0, 4096)
    hot_group = forced[:, None] & (node_ids[None, :] == (hot_expert // N_LOCAL)[:, None])
    group_score = group_score + 8192 * hot_group.astype(jnp.int32)
    _, group_ids = lax.top_k(group_score * N_NODE + node_ids[None, :], GROUPS_TOK)
    chosen = jnp.any(group_ids[:, :, None] == node_ids[None, None, :], axis=1)
    expert_index = jnp.arange(EXPERTS, dtype=jnp.int32)
    popularity = jax.random.randint(split_keys[4], (EXPERTS,), 0, 1024)
    base_score = jax.random.randint(split_keys[3], (TOKENS, EXPERTS), 0, 4096) + popularity[None, :]
    local_index = jnp.arange(N_LOCAL, dtype=jnp.int32)
    within = base_score.reshape(TOKENS, N_NODE, N_LOCAL) * N_LOCAL + local_index
    leader = (within == jnp.max(within, axis=2, keepdims=True)).reshape(TOKENS, EXPERTS)
    allowed = chosen[:, expert_index // N_LOCAL]
    hot_pick = forced[:, None] & (expert_index[None, :] == hot_expert[:, None])
    score_boost = 8192 * leader.astype(jnp.int32) + 16384 * hot_pick.astype(jnp.int32)
    expert_score = jnp.where(allowed, base_score + 1 + score_boost, 0)
    _, expert_ids = lax.top_k(expert_score * EXPERTS + expert_index[None, :], TOPK)
    per_block = block_tokens * TOPK
    blocked = jnp.transpose(expert_ids.reshape(N_NODE, N_LOCAL, N_DP, TOK_DEV, TOPK), (1, 2, 0, 3, 4)).reshape(N_LOCAL * N_DP, per_block)
    positions = jnp.arange(per_block, dtype=jnp.int32)
    sort_order = jnp.argsort(blocked * per_block + positions[None, :], axis=1)
    sorted_ids = jnp.take_along_axis(blocked, sort_order, axis=1)
    starts = jnp.concatenate([jnp.ones((N_LOCAL * N_DP, 1), dtype=bool), sorted_ids[:, 1:] != sorted_ids[:, :-1]], axis=1)
    run_start = lax.cummax(jnp.where(starts, positions[None, :], 0), axis=1)
    sorted_rank = positions[None, :] - run_start
    slot_rank = jnp.take_along_axis(sorted_rank, jnp.argsort(sort_order, axis=1), axis=1)
    slot_table = jnp.where(slot_rank < CAP_BLOCK, slot_rank, -1)
    slot_table = jnp.transpose(slot_table.reshape(N_LOCAL, N_DP, N_NODE, TOK_DEV, TOPK), (2, 0, 1, 3, 4)).reshape(TOKENS, TOPK)
    return (expert_ids.astype(jnp.int32), slot_table.astype(jnp.int32))


def draw_expert_ids(key, part):
    return routing(key)[0]


def draw_slot_ids(key, part):
    return routing(key)[1]


def block_levels(key, dims, cuts, least, high):
    def one(dim, parts):
        heights = jax.random.uniform(jax.random.fold_in(jax.random.fold_in(key, 6), dim), (parts,), jnp.float32, least / len(cuts), high / len(cuts))
        return jnp.repeat(jnp.exp(heights), dims[dim] // parts).reshape((-1,) + (1,) * (len(dims) - dim - 1))

    level = one(*cuts[0])
    for cut in cuts[1:]:
        level = level * one(*cut)
    return level


def gaussian(stream_key, shape, width, reach, pieces=(), held_as=jnp.bfloat16):
    loudness = block_levels(stream_key, shape, pieces, -0.22, 0.18) if pieces else 1.0
    array = jax.random.normal(stream_key, shape, jnp.float32) * width * loudness
    return jnp.minimum(jnp.maximum(array, -reach), reach).astype(held_as)


def setup_inputs(seed: int = 0) -> dict:
    key_of = jax.random.split(jax.random.key(seed), 6)
    return {
        "grad_out": gaussian(key_of[0], (TOKENS, D), 1.0, 6.0, ((0, 1024),)),
        "expert_ids": draw_expert_ids(jax.random.fold_in(key_of[5], 71), 0),
        "slot_ids": draw_slot_ids(jax.random.fold_in(key_of[5], 71), 0),
        "gate_values": jnp.clip(0.049804688 + 0.54785156 * jax.random.uniform(key_of[3], (TOKENS, TOPK), jnp.float32) ** block_levels(key_of[3], (TOKENS, TOPK), ((0, 1024),), -0.2, 0.2), 0.049804688, 0.59765625).astype(jnp.bfloat16),
        "hidden": gaussian(key_of[4], (EXPERTS, N_DP * CAPACITY, FF), 0.1, 0.59765625, ((0, 256), (1, 4))),
    }


def reference(grad_out, expert_ids, slot_ids, gate_values, hidden):
    tokens = jnp.arange(TOKENS, dtype=jnp.int32)
    device = tokens // TOK_DEV
    local_index = (device // N_DP) % N_LOCAL
    replica = device % N_DP
    kept_slot = slot_ids >= 0
    position = replica[:, None] * CAPACITY + local_index[:, None] * CAP_BLOCK + slot_ids
    slot_total = EXPERTS * N_DP * CAPACITY
    flat_index = jnp.where(kept_slot, expert_ids * (N_DP * CAPACITY) + position, slot_total).reshape(-1).astype(jnp.int32)
    owners = jnp.broadcast_to(tokens[:, None], expert_ids.shape).reshape(-1)
    source = jnp.full((slot_total,), -1, jnp.int32).at[flat_index].set(owners, mode="drop")
    slot_gates = jnp.zeros((slot_total,), gate_values.dtype).at[flat_index].set(gate_values.reshape(-1), mode="drop")
    source = source.reshape(EXPERTS, N_DP, CAPACITY)
    slot_gates = slot_gates.reshape(EXPERTS, N_DP, CAPACITY)

    def one_expert(operands):
        rows_source, gate_slots, hidden_rows = operands
        picked = grad_out[jnp.maximum(rows_source, 0)]
        expert_rows = jnp.where((rows_source >= 0)[:, :, None], picked, jnp.zeros((), grad_out.dtype))
        scaled = (gate_slots.astype(jnp.float32)[:, :, None] * hidden_rows.reshape(N_DP, CAPACITY, FF).astype(jnp.float32)).astype(jnp.bfloat16)
        partials = jnp.einsum("rcd,rcf->rdf", expert_rows.astype(jnp.float32), scaled.astype(jnp.float32))
        partials = lax.optimization_barrier(partials.astype(jnp.bfloat16)).astype(jnp.float32)
        return jnp.sum(partials, axis=0).astype(jnp.bfloat16)

    return lax.map(one_expert, (source, slot_gates, hidden))
```

```python
import jax
import jax.numpy as jnp
from jax import lax
from jax.experimental import pallas as pl
from jax.experimental.pallas import tpu as pltpu
from jax.sharding import PartitionSpec as P

MESH = pl.DeviceIdType.MESH
LANES = 128
TOK_PAD = 32
META = 32
CHUNKS = 2


def remote(src, dst, send_sem, recv_sem, **device):
    return pltpu.make_async_remote_copy(
        src_ref=src,
        dst_ref=dst,
        send_sem=send_sem,
        recv_sem=recv_sem,
        device_id=device,
        device_id_type=MESH,
    )


def kernel(
    rows_ref,
    ids_ref,
    slots_ref,
    gates_ref,
    hidden_ref,
    out_ref,
    ystage,
    yrecv,
    zbuf,
    near,
    far,
    far_in,
    relay_in,
    direct_in,
    bucket,
    hid_all,
    hid_perm,
    acc,
    y_send,
    y_recv,
    h_send,
    h_recv,
    h_local,
    z_send,
    z_recv,
    f_send,
    f_recv,
    r_send,
    r_recv,
    d_send,
    d_recv,
):
    bf16, f32 = jnp.bfloat16, jnp.float32
    node, z, y = lax.axis_index("node"), lax.axis_index("local"), lax.axis_index("dp")
    n_z, n_y = lax.axis_size("local"), lax.axis_size("dp")
    n_x = lax.axis_size("node") // 2
    x, core = node // 2, lax.rem(node, 2)
    sibling = x * 2 + (1 - core)
    x_up, x_down = lax.rem(x + 1, n_x), lax.rem(x + n_x - 1, n_x)
    z_up, z_down = lax.rem(z + 1, n_z), lax.rem(z + n_z - 1, n_z)
    n_tok = rows_ref.shape[0]
    half = n_z // 2
    feats = out_ref.shape[0]
    n_col = feats // LANES
    tokens = n_y * n_tok
    data_rows = n_col * tokens
    chunk = (data_rows + META) // CHUNKS
    slots = hidden_ref.shape[0] // n_z
    per_block = n_y * slots
    pair = 2 * per_block
    top = ids_ref.shape[1]

    barrier = pltpu.get_barrier_semaphore()
    greet = [{"dp": lax.rem(y + d, n_y)} for d in range(1, n_y)]
    greet += [{"local": z_up}, {"local": z_down}, {"node": sibling}]
    greet += [{"node": x_up * 2 + core}, {"node": x_down * 2 + core}]
    for device in greet:
        pl.semaphore_signal(barrier, inc=1, device_id=device, device_id_type=MESH)

    ystage[...] = jnp.zeros_like(ystage)
    put = (
        lax.broadcasted_iota(jnp.int32, (n_tok, LANES), 1)
        == lax.broadcasted_iota(jnp.int32, (n_tok, LANES), 0) + y * n_tok
    ).astype(bf16)

    def on_lanes(values):
        return lax.dot_general(
            values.astype(f32).astype(bf16),
            put,
            (((0,), (0,)), ((), ())),
            preferred_element_type=f32,
        )

    slot_values = slots_ref[...]
    position = jnp.where(slot_values >= 0, slot_values + y * slots, 31)
    meta = jnp.concatenate(
        [
            on_lanes(ids_ref[...]),
            on_lanes(position),
            on_lanes(gates_ref[...]),
            jnp.zeros((META - 3 * top, LANES), f32),
        ],
        axis=0,
    ).astype(bf16)
    for part in range(n_y):
        ystage[part, :n_tok, :feats] = rows_ref[:, part * feats : (part + 1) * feats]
        ystage[part, :, feats:] = meta

    pl.semaphore_wait(barrier, len(greet))

    def y_copy(d):
        peer = lax.rem(y + d, n_y)
        return remote(
            ystage.at[peer], yrecv.at[y], y_send.at[d - 1], y_recv.at[d - 1], dp=peer
        )

    for d in range(1, n_y):
        y_copy(d).start()
    yrecv[y] = ystage[y]

    def y_arrival(d):
        sender = lax.rem(y + n_y - d, n_y)
        return remote(
            ystage.at[sender], yrecv.at[sender], y_send.at[d - 1], y_recv.at[d - 1], dp=sender
        )

    for d in range(1, n_y):
        y_arrival(d).wait_recv()

    to = lax.broadcasted_iota(jnp.int32, (tokens, n_y * TOK_PAD), 0)
    of = lax.broadcasted_iota(jnp.int32, (tokens, n_y * TOK_PAD), 1)
    pick = jnp.zeros((tokens, n_y * TOK_PAD), jnp.bool_)
    for part in range(n_y):
        pick = pick | (
            (of - part * TOK_PAD == to - part * n_tok)
            & (of >= part * TOK_PAD)
            & (of < part * TOK_PAD + n_tok)
        )
    arrived = yrecv[...].reshape(n_y * TOK_PAD, feats + LANES)
    block = jnp.dot(
        pick.astype(bf16), arrived[:, :feats], preferred_element_type=f32
    ).astype(bf16)
    for j in range(n_col):
        zbuf[0, 0, j * tokens : (j + 1) * tokens, :] = block[:, j * LANES : (j + 1) * LANES]
    total = yrecv[0, :, feats:].astype(f32)
    for part in range(1, n_y):
        total = total + yrecv[part, :, feats:].astype(f32)
    zbuf[0, 0, data_rows:, :] = total.astype(bf16)

    def z_copy(side, slot, to_side, to_slot, c):
        piece = pl.ds(c * chunk, chunk)
        return remote(
            zbuf.at[side, slot, piece],
            zbuf.at[to_side, to_slot, piece],
            z_send.at[side, slot, c],
            z_recv.at[to_side, to_slot, c],
            local=z_up if side == 0 else z_down,
        )

    def z_own(side, c):
        piece = pl.ds(c * chunk, chunk)
        return remote(
            zbuf.at[0, 0, piece],
            zbuf.at[side, 1, piece],
            z_send.at[side, 0, c],
            z_recv.at[side, 1, c],
            local=z_up if side == 0 else z_down,
        )

    for c in range(CHUNKS):
        for side in range(2):
            z_own(side, c).start()

    def h_copy(d):
        peer = lax.rem(y + d, n_y)
        return remote(
            hidden_ref, hid_all.at[y], h_send.at[d - 1], h_recv.at[d - 1], dp=peer
        )

    def h_arrival(d):
        sender = lax.rem(y + n_y - d, n_y)
        return remote(
            hidden_ref, hid_all.at[sender], h_send.at[d - 1], h_recv.at[d - 1], dp=sender
        )

    for d in range(1, n_y):
        h_copy(d).start()
    own_hidden = pltpu.make_async_copy(hidden_ref, hid_all.at[y], h_local)
    own_hidden.start()

    def far_copy(b):
        return remote(far.at[b], far_in.at[b], f_send.at[b], f_recv.at[b], node=sibling)

    def direction(b):
        up = lax.rem(b, 2) == 0
        return jnp.where(up, x_up, x_down), jnp.where(up, x_down, x_up)

    def relay_copy(b):
        ahead, _ = direction(b)
        opposite = lax.rem(x + 2, n_x)
        return remote(
            near.at[b, opposite],
            relay_in.at[b],
            r_send.at[b],
            r_recv.at[b],
            node=ahead * 2 + core,
        )

    def direct_copy(b, target, lane):
        return remote(
            near.at[b, target],
            direct_in.at[b, lane],
            d_send.at[b, lane],
            d_recv.at[b, lane],
            node=target * 2 + core,
        )

    def lanes_of(b):
        up = lax.rem(b, 2) == 0
        return jnp.where(up, 0, 1), jnp.where(up, 1, 0)

    row = lax.broadcasted_iota(jnp.int32, (n_x, per_block, LANES), 0)
    place_in = lax.broadcasted_iota(jnp.int32, (n_x, per_block, LANES), 1)

    def place(t):
        slot = lax.rem(t, half)
        b = t - 1
        codes, gates = [], []
        sides = []
        for side in range(2):
            routing = zbuf[side, slot, data_rows:, :].astype(f32)
            codes.append(routing[:top] * 32.0 + routing[top : 2 * top])
            gates.append(routing[2 * top : 3 * top])
            sides += [
                jnp.concatenate(
                    [
                        zbuf[side, slot, j * tokens : (j + 1) * tokens, :]
                        for j in range(n_col)
                    ],
                    axis=1,
                ),
                jnp.zeros((LANES - tokens, feats), bf16),
            ]
        values = jnp.concatenate(sides, axis=0)
        for which, dest in ((1 - core, far), (core, near)):
            target = (((row * 2 + which) * n_z + z) * 32 + place_in).astype(f32)
            parts = []
            for side in range(2):
                weight = jnp.zeros((n_x, per_block, LANES), f32)
                for k in range(top):
                    weight = weight + jnp.where(
                        codes[side][k : k + 1, :][None] == target,
                        gates[side][k : k + 1, :][None],
                        0.0,
                    )
                blank = jnp.zeros_like(weight)
                both = (weight, blank) if side == 0 else (blank, weight)
                parts.append(jnp.concatenate(both, axis=1).reshape(n_x * pair, LANES))
            placement = jnp.concatenate(parts, axis=1).astype(bf16)
            placed = jnp.dot(placement, values, preferred_element_type=f32)
            dest[b] = placed.astype(bf16).reshape(n_x, pair, feats)
            if dest is far:
                far_copy(b).start()

    def merge_core(t):
        b = t - 1
        far_copy(b).wait_recv()
        near[b] = near[b] + far_in[b]
        relay_copy(b).start()
        _, behind = direction(b)
        _, lane = lanes_of(b)
        direct_copy(b, behind, lane).start()

    def merge_relay(t):
        b = t - 1
        relay_copy(b).wait_recv()
        ahead, _ = direction(b)
        lane, _ = lanes_of(b)
        near[b, ahead] = near[b, ahead] + relay_in[b]
        direct_copy(b, ahead, lane).start()

    def finish(t):
        b = t - 1
        direct_copy(b, x_up, 0).wait_recv()
        direct_copy(b, x_down, 1).wait_recv()
        bucket[b] = near[b, x] + direct_in[b, 0] + direct_in[b, 1]

    group_pairs = half // 4
    group = group_pairs * pair

    def order_hidden():
        for d in range(1, n_y):
            h_arrival(d).wait_recv()
        own_hidden.wait()
        wide = (group, n_y * n_z * slots)

        @pl.loop(0, 4)
        def _(g):
            i = lax.broadcasted_iota(jnp.int32, (group, 1), 0)
            step = lax.div(i, pair) + g * group_pairs + 1
            side = lax.rem(lax.div(i, per_block), 2)
            at = lax.rem(i, per_block)
            source = jnp.where(side == 0, z - lax.rem(step, half), z + step)
            source = lax.rem(source + n_z, n_z)
            replica = lax.div(at, slots)
            column = replica * (n_z * slots) + source * slots + (at - replica * slots)
            choose = (lax.broadcasted_iota(jnp.int32, wide, 1) == column).astype(bf16)
            hid_perm[g] = jnp.dot(
                choose,
                hid_all[...].reshape(wide[1], hid_all.shape[2]),
                preferred_element_type=f32,
            ).astype(bf16)

    def product(g, first, last):
        @pl.loop(0, n_col)
        def _(j):
            cols = pl.ds(pl.multiple_of(j * LANES, LANES), LANES)
            left = bucket[g * group_pairs : (g + 1) * group_pairs, :, cols]
            term = lax.dot_general(
                left.reshape(group, LANES),
                hid_perm[g],
                (((0,), (0,)), ((), ())),
                preferred_element_type=f32,
            )
            if not first:
                term = term + acc[cols, :]
            if last:
                out_ref[cols, :] = term.astype(bf16)
            else:
                acc[cols, :] = term

    def z_step(t, c):
        for side in range(2):
            z_copy(side, t - 1, side, t, c).wait_recv()

            @pl.when(t < half - 1)
            def _():
                z_copy(side, t, side, t + 1, c).start()

            if side == c:

                @pl.when(t == half - 1)
                def _():
                    z_copy(side, t, 1, 0, c).start()

    @pl.loop(1, half + 4)
    def _(t):
        @pl.when(t < half)
        def _():
            z_step(t, 0)

        @pl.when((t > 1) & (t <= half + 1))
        def _():
            merge_core(t - 1)

        @pl.when((t > 2) & (t <= half + 2))
        def _():
            merge_relay(t - 2)

        @pl.when(t < half)
        def _():
            z_step(t, 1)

        @pl.when(t == half)
        def _():
            for c in range(CHUNKS):
                z_copy(c, half - 1, 1, 0, c).wait_recv()

        @pl.when(t <= half)
        def _():
            place(t)

        @pl.when(t > 3)
        def _():
            finish(t - 3)

        @pl.when(t == half // 2)
        def _():
            order_hidden()

        for g in range(3):

            @pl.when(t == max(half // 2 + 1, group_pairs * (g + 1) + 3) + (g == 1))
            def _():
                product(g, g == 0, False)

    product(3, False, True)

    for d in range(1, n_y):
        y_copy(d).wait_send()
        h_copy(d).wait_send()
    for c in range(CHUNKS):
        for side in range(2):
            z_own(side, c).wait_send()

            @pl.loop(1, half - 1)
            def _(t):
                z_copy(side, t, side, t + 1, c).wait_send()

        z_copy(c, half - 1, 1, 0, c).wait_send()

    @pl.loop(0, half)
    def _(b):
        far_copy(b).wait_send()
        relay_copy(b).wait_send()
        direct_copy(b, x_up, 0).wait_send()
        direct_copy(b, x_down, 1).wait_send()


def shards(grad_out, expert_ids, slot_ids, gate_values, hidden):
    n_x = lax.axis_size("node") // 2
    n_z, n_y = lax.axis_size("local"), lax.axis_size("dp")
    n_tok, width = grad_out.shape
    _, capacity, units = hidden.shape
    feats = width // n_y
    half = n_z // 2
    pair = 2 * n_y * capacity // n_z
    block_rows = feats // LANES * n_y * n_tok + META
    bf16 = jnp.bfloat16
    vmem = pl.BlockSpec(memory_space=pltpu.VMEM)
    dma = pltpu.SemaphoreType.DMA
    result = pl.pallas_call(
        kernel,
        out_shape=jax.ShapeDtypeStruct((feats, units), bf16),
        in_specs=[vmem] * 4 + [pl.BlockSpec(memory_space=pl.ANY)],
        out_specs=vmem,
        scratch_shapes=[
            pltpu.VMEM((n_y, TOK_PAD, feats + LANES), bf16),
            pltpu.VMEM((n_y, TOK_PAD, feats + LANES), bf16),
            pltpu.VMEM((2, half, block_rows, LANES), bf16),
            pltpu.VMEM((half, n_x, pair, feats), bf16),
            pltpu.VMEM((half, n_x, pair, feats), bf16),
            pltpu.VMEM((half, n_x, pair, feats), bf16),
            pltpu.VMEM((half, pair, feats), bf16),
            pltpu.VMEM((half, 2, pair, feats), bf16),
            pltpu.VMEM((half, pair, feats), bf16),
            pltpu.VMEM((n_y, capacity, units), bf16),
            pltpu.VMEM((4, half // 4 * pair, units), bf16),
            pltpu.VMEM((feats, units), jnp.float32),
            dma((n_y - 1,)),
            dma((n_y - 1,)),
            dma((n_y - 1,)),
            dma((n_y - 1,)),
            dma,
            dma((2, half, CHUNKS)),
            dma((2, half, CHUNKS)),
            dma((half,)),
            dma((half,)),
            dma((half,)),
            dma((half,)),
            dma((half, 2)),
            dma((half, 2)),
        ],
        compiler_params=pltpu.CompilerParams(
            collective_id=0, has_side_effects=True, vmem_limit_bytes=56 * 1024 * 1024
        ),
        cost_estimate=pl.CostEstimate(
            flops=2 * n_y * capacity * feats * units, bytes_accessed=4 << 20, transcendentals=0
        ),
    )(grad_out, expert_ids, slot_ids, gate_values, hidden[0])
    return result[None]


def solution(mesh):
    in_specs = (
        P(("node", "local", "dp"), None),
        P(("node", "local", "dp"), None),
        P(("node", "local", "dp"), None),
        P(("node", "local", "dp"), None),
        P(("node", "local"), "dp", None),
    )
    out_specs = P(("node", "local"), "dp", None)
    return jax.shard_map(shards, mesh=mesh, in_specs=in_specs, out_specs=out_specs, check_vma=False)
```

```python
import jax
import jax.numpy as jnp
from jax import lax
from jax.experimental import pallas as pl
from jax.experimental.pallas import tpu as pltpu
from jax.sharding import PartitionSpec as P

MESH = pl.DeviceIdType.MESH
LANES = 128
CODE = 32
ONE = 32
GROUPS = 3


def remote(src, dst, send_sem, recv_sem, **device):
    return pltpu.make_async_remote_copy(
        src_ref=src,
        dst_ref=dst,
        send_sem=send_sem,
        recv_sem=recv_sem,
        device_id=device,
        device_id_type=MESH,
    )


def kernel(
    rows_ref,
    ids_ref,
    slots_ref,
    gates_ref,
    hidden_ref,
    out_ref,
    stage,
    zbuf,
    near,
    far,
    far_in,
    relay_in,
    direct_in,
    near_one,
    far_one,
    far_one_in,
    direct_one_in,
    bucket,
    bucket_one,
    hid_all,
    hid_perm,
    hid_one,
    acc,
    y_send,
    y_recv,
    h_send,
    h_recv,
    h_local,
    z_send,
    z_recv,
    f_send,
    f_recv,
    r_send,
    r_recv,
    d_send,
    d_recv,
    e_send,
    e_recv,
):
    bf16, f32 = jnp.bfloat16, jnp.float32
    node, z, y = lax.axis_index("node"), lax.axis_index("local"), lax.axis_index("dp")
    n_z, n_y = lax.axis_size("local"), lax.axis_size("dp")
    n_x = lax.axis_size("node") // 2
    x, core = node // 2, lax.rem(node, 2)
    sibling = x * 2 + (1 - core)
    x_up, x_down = lax.rem(x + 1, n_x), lax.rem(x + n_x - 1, n_x)
    z_up, z_down = lax.rem(z + 1, n_z), lax.rem(z + n_z - 1, n_z)
    n_tok = rows_ref.shape[0]
    half = n_z // 2
    last = half - 1
    feats = out_ref.shape[0]
    n_col = feats // LANES
    top = ids_ref.shape[0]
    data_rows = n_col * n_tok
    piece = data_rows + top
    lane_group = LANES // n_y
    slots = hidden_ref.shape[0] // n_z
    per_block = n_y * slots
    pair = 2 * per_block

    barrier = pltpu.get_barrier_semaphore()
    opposite = lax.rem(x + 2, n_x)
    greet = [{"dp": lax.rem(y + d, n_y)} for d in range(1, n_y)]
    greet += [{"local": z_up}, {"local": z_down}, {"node": sibling}]
    greet += [{"node": chip * 2 + core} for chip in (x_up, x_down, opposite)]
    for device in greet:
        pl.semaphore_signal(barrier, inc=1, device_id=device, device_id_type=MESH)

    def on_lanes(values, group):
        put = lax.broadcasted_iota(jnp.int32, (n_tok, LANES), 1) == (
            lax.broadcasted_iota(jnp.int32, (n_tok, LANES), 0) + group * lane_group
        )
        return jnp.dot(
            values.astype(f32).astype(bf16), put.astype(bf16), preferred_element_type=f32
        )

    slot_values = slots_ref[...]
    position = jnp.where(slot_values >= 0, slot_values + y * slots, CODE - 1)
    routing = on_lanes(ids_ref[...], 0) + on_lanes(position, 1) + on_lanes(gates_ref[...], 2)

    def piece_rows(k):
        return pl.ds(k * piece, piece)

    for d in range(n_y):
        k = (n_y - d) % n_y
        peer = lax.rem(y + d, n_y)
        columns = [
            rows_ref[:, pl.ds(pl.multiple_of(peer * feats + j * LANES, LANES), LANES)].astype(f32)
            for j in range(n_col)
        ]
        columns.append(pltpu.roll(routing, k * lane_group, 1) if k else routing)
        whole = jnp.concatenate(columns, axis=0).astype(bf16)
        if d == 0:
            zbuf[0, 0, :piece, :] = whole
        else:
            stage[d - 1] = whole

    pl.semaphore_wait(barrier, len(greet))

    def y_copy(d):
        return remote(
            stage.at[d - 1],
            zbuf.at[0, 0, piece_rows(n_y - d)],
            y_send.at[d - 1],
            y_recv.at[d - 1],
            dp=lax.rem(y + d, n_y),
        )

    def z_copy(side, slot, to_side, to_slot, k):
        return remote(
            zbuf.at[side, slot, piece_rows(k)],
            zbuf.at[to_side, to_slot, piece_rows(k)],
            z_send.at[side, slot, k],
            z_recv.at[to_side, to_slot, k],
            local=z_up if side == 0 else z_down,
        )

    def z_own(side, k):
        return remote(
            zbuf.at[0, 0, piece_rows(k)],
            zbuf.at[side, 1, piece_rows(k)],
            z_send.at[side, 0, k],
            z_recv.at[side, 1, k],
            local=z_up if side == 0 else z_down,
        )

    for d in (1, n_y - 1, 2):
        y_copy(d).start()
    for side in range(2):
        z_own(side, 0).start()
    y_copy(n_y - 1).wait_recv()
    z_own(0, 1).start()
    y_copy(1).wait_recv()
    z_own(1, 3).start()
    z_own(0, 3).start()
    y_copy(2).wait_recv()
    z_own(1, 2).start()
    z_own(0, 2).start()
    z_own(1, 1).start()
    order = ((0, 1, 3, 2), (0, 3, 2, 1))
    to_opposite = ((0, 1), (3, 2))

    def h_copy(d):
        return remote(
            hidden_ref,
            hid_all.at[y],
            h_send.at[d - 1],
            h_recv.at[d - 1],
            dp=lax.rem(y + d, n_y),
        )

    def h_arrival(d):
        sender = lax.rem(y + n_y - d, n_y)
        return remote(
            hidden_ref, hid_all.at[sender], h_send.at[d - 1], h_recv.at[d - 1], dp=sender
        )

    for d in range(1, n_y):
        h_copy(d).start()
    own_hidden = pltpu.make_async_copy(hidden_ref, hid_all.at[y], h_local)
    own_hidden.start()

    def far_copy(b):
        return remote(far.at[b], far_in.at[b], f_send.at[b], f_recv.at[b], node=sibling)

    def far_one_copy(s):
        return remote(
            far_one.at[s],
            far_one_in.at[s],
            f_send.at[last + s],
            f_recv.at[last + s],
            node=sibling,
        )

    cut = (n_col + 1) // 2 * LANES
    ways = ((x_up, slice(0, cut)), (x_down, slice(cut, feats)))

    def relay_copy(b, way):
        ahead, cols = ways[way]
        return remote(
            near.at[b, opposite, :, cols],
            relay_in.at[b, :, cols],
            r_send.at[b, way],
            r_recv.at[b, way],
            node=ahead * 2 + core,
        )

    def direct_copy(b, way):
        ahead, _ = ways[way]
        return remote(
            near.at[b, ahead],
            direct_in.at[b, way],
            d_send.at[b, way],
            d_recv.at[b, way],
            node=ahead * 2 + core,
        )

    def direct_one_copy(s, way):
        chip = (x_up, x_down, opposite)[way]
        return remote(
            near_one.at[s, chip],
            direct_one_in.at[s, way],
            e_send.at[s, way],
            e_recv.at[s, way],
            node=chip * 2 + core,
        )

    row = lax.broadcasted_iota(jnp.int32, (n_x, per_block, LANES), 0)
    place_in = lax.broadcasted_iota(jnp.int32, (n_x, per_block, LANES), 1)
    lane_of = lax.broadcasted_iota(jnp.int32, (top, LANES), 1) // lane_group

    def read_block(side, slot):
        block = zbuf[side, slot].astype(f32)
        gap = jnp.zeros((lane_group - n_tok, LANES), f32)
        columns = []
        for j in range(n_col):
            rows = []
            for k in range(n_y):
                start = k * piece + j * n_tok
                rows += [block[start : start + n_tok], gap]
            columns.append(jnp.concatenate(rows, axis=0))
        values = jnp.concatenate(columns, axis=1).astype(bf16)
        parts = []
        for shift in range(3):
            part = jnp.zeros((top, LANES), f32)
            for k in range(n_y):
                held = block[k * piece + data_rows : (k + 1) * piece]
                part = jnp.where(lane_of == (k + shift) % n_y, held, part)
            parts.append(
                pltpu.roll(part, LANES - shift * lane_group, 1) if shift else part
            )
        return values, parts[0] * float(CODE) + parts[1], parts[2]

    def weights(codes, gates, which):
        target = (((row * 2 + which) * n_z + z) * CODE + place_in).astype(f32)
        weight = jnp.zeros((n_x, per_block, LANES), f32)
        for k in range(top):
            weight = weight + jnp.where(
                codes[k : k + 1, :][None] == target, gates[k : k + 1, :][None], 0.0
            )
        return weight

    def place(t):
        b = t - 1
        blocks = [read_block(side, t) for side in range(2)]
        values = jnp.concatenate([values for values, _, _ in blocks], axis=0)
        for which, dest in ((1 - core, far), (core, near)):
            parts = []
            for side in range(2):
                weight = weights(*blocks[side][1:], which)
                blank = jnp.zeros_like(weight)
                both = (weight, blank) if side == 0 else (blank, weight)
                parts.append(jnp.concatenate(both, axis=1).reshape(n_x * pair, LANES))
            placement = jnp.concatenate(parts, axis=1).astype(bf16)
            placed = jnp.dot(placement, values, preferred_element_type=f32)
            dest[b] = placed.astype(bf16).reshape(n_x, pair, feats)
            if dest is far:
                far_copy(b).start()

    def place_one(s):
        values, codes, gates = read_block(s, 0)
        gap = jnp.zeros((n_x, ONE - per_block, LANES), f32)
        for which, dest in ((1 - core, far_one), (core, near_one)):
            weight = jnp.concatenate([weights(codes, gates, which), gap], axis=1)
            placed = jnp.dot(
                weight.reshape(n_x * ONE, LANES).astype(bf16),
                values,
                preferred_element_type=f32,
            )
            dest[s] = placed.astype(bf16).reshape(n_x, ONE, feats)
            if dest is far_one:
                far_one_copy(s).start()

    def merge_core(t):
        b = t - 1
        far_copy(b).wait_recv()
        near[b, opposite] = near[b, opposite] + far_in[b, opposite]
        for way in range(2):
            relay_copy(b, way).start()
        for chip in (x_up, x_down, x):
            near[b, chip] = near[b, chip] + far_in[b, chip]

    def merge_relay(t):
        b = t - 1
        for way in range(2):
            ahead, cols = ways[way]
            relay_copy(b, way).wait_recv()
            near[b, ahead, :, cols] = near[b, ahead, :, cols] + relay_in[b, :, cols]
            direct_copy(b, way).start()

    def finish(t):
        b = t - 1
        for way in range(2):
            direct_copy(b, way).wait_recv()
        bucket[b] = near[b, x] + direct_in[b, 0] + direct_in[b, 1]

    def merge_one(s):
        far_one_copy(s).wait_recv()
        for way, chip in ((2, opposite), (0, x_up), (1, x_down)):
            near_one[s, chip] = near_one[s, chip] + far_one_in[s, chip]
            direct_one_copy(s, way).start()
        near_one[s, x] = near_one[s, x] + far_one_in[s, x]

    def finish_one(s):
        total = near_one[s, x]
        for way in range(3):
            direct_one_copy(s, way).wait_recv()
            total = total + direct_one_in[s, way]
        bucket_one[s] = total

    group_pairs = last // GROUPS
    group = group_pairs * pair
    positions = n_y * n_z * slots

    def choose(count, source, at):
        replica = lax.div(at, slots)
        column = replica * (n_z * slots) + source * slots + (at - replica * slots)
        pick = lax.broadcasted_iota(jnp.int32, (count, positions), 1) == column
        return jnp.dot(
            pick.astype(bf16),
            hid_all[...].reshape(positions, hid_all.shape[2]),
            preferred_element_type=f32,
        ).astype(bf16)

    def order_hidden():
        for d in range(1, n_y):
            h_arrival(d).wait_recv()
        own_hidden.wait()

        @pl.loop(0, GROUPS)
        def _(g):
            i = lax.broadcasted_iota(jnp.int32, (group, 1), 0)
            step = lax.div(i, pair) + g * group_pairs + 1
            side = lax.rem(lax.div(i, per_block), 2)
            source = lax.rem(jnp.where(side == 0, z - step, z + step) + n_z, n_z)
            hid_perm[g] = choose(group, source, lax.rem(i, per_block))

        i = lax.broadcasted_iota(jnp.int32, (2 * ONE, 1), 0)
        source = lax.rem(z + jnp.where(i < ONE, 0, half), n_z)
        at = jnp.where(i < ONE, i, i - ONE)
        hid_one[...] = choose(2 * ONE, source, jnp.where(at < per_block, at, positions))

    def product(g):
        @pl.loop(0, n_col)
        def _(j):
            cols = pl.ds(pl.multiple_of(j * LANES, LANES), LANES)
            if g < GROUPS:
                left = bucket[g * group_pairs : (g + 1) * group_pairs, :, cols]
                left, right = left.reshape(group, LANES), hid_perm[g]
            else:
                left, right = bucket_one[:, :, cols].reshape(2 * ONE, LANES), hid_one[...]
            term = lax.dot_general(
                left, right, (((0,), (0,)), ((), ())), preferred_element_type=f32
            )
            if g > 0:
                term = term + acc[cols, :]
            if g < GROUPS:
                acc[cols, :] = term
            else:
                out_ref[cols, :] = term.astype(bf16)

    place_one(0)

    @pl.loop(1, half)
    def _(t):
        def z_step(at):
            for side in range(2):
                k = order[side][at]
                z_copy(side, t - 1, side, t, k).wait_recv()

                @pl.when(t < last)
                def _():
                    z_copy(side, t, side, t + 1, k).start()

                if k in to_opposite[side]:

                    @pl.when(t == last)
                    def _():
                        z_copy(side, t, 1, 0, k).start()

        z_step(0)
        z_step(1)

        @pl.when(t == 1)
        def _():
            merge_one(0)

        @pl.when(t > 1)
        def _():
            merge_core(t - 1)

        @pl.when(t > 2)
        def _():
            merge_relay(t - 2)

        z_step(2)
        z_step(3)
        place(t)

        @pl.when(t == 3)
        def _():
            finish_one(0)

        @pl.when(t > 3)
        def _():
            finish(t - 3)

        @pl.when(t == half // 2)
        def _():
            order_hidden()

        for g in range(GROUPS - 1):

            @pl.when(t == max(half // 2 + 1, group_pairs * (g + 1) + 3))
            def _():
                product(g)

    merge_core(last)
    merge_relay(last - 1)
    finish(last - 2)
    for side in range(2):
        for k in to_opposite[side]:
            z_copy(side, last, 1, 0, k).wait_recv()
    place_one(1)
    merge_relay(last)
    merge_one(1)
    finish(last - 1)
    finish(last)
    product(GROUPS - 1)
    finish_one(1)
    product(GROUPS)

    for d in range(1, n_y):
        y_copy(d).wait_send()
        h_copy(d).wait_send()
    for k in range(n_y):
        for side in range(2):
            z_own(side, k).wait_send()

            @pl.loop(1, last)
            def _(t):
                z_copy(side, t, side, t + 1, k).wait_send()

            if k in to_opposite[side]:
                z_copy(side, last, 1, 0, k).wait_send()

    @pl.loop(0, last)
    def _(b):
        far_copy(b).wait_send()
        for way in range(2):
            relay_copy(b, way).wait_send()
            direct_copy(b, way).wait_send()

    for s in range(2):
        far_one_copy(s).wait_send()
        for way in range(3):
            direct_one_copy(s, way).wait_send()


def shards(grad_out, expert_ids, slot_ids, gate_values, hidden):
    n_x = lax.axis_size("node") // 2
    n_z, n_y = lax.axis_size("local"), lax.axis_size("dp")
    n_tok, width = grad_out.shape
    top = expert_ids.shape[1]
    _, capacity, units = hidden.shape
    feats = width // n_y
    half = n_z // 2
    last = half - 1
    pair = 2 * n_y * capacity // n_z
    piece = feats // LANES * n_tok + top
    bf16 = jnp.bfloat16
    vmem = pl.BlockSpec(memory_space=pltpu.VMEM)
    dma = pltpu.SemaphoreType.DMA
    result = pl.pallas_call(
        kernel,
        out_shape=jax.ShapeDtypeStruct((feats, units), bf16),
        in_specs=[vmem] * 4 + [pl.BlockSpec(memory_space=pl.ANY)],
        out_specs=vmem,
        scratch_shapes=[
            pltpu.VMEM((n_y - 1, piece, LANES), bf16),
            pltpu.VMEM((2, half, n_y * piece, LANES), bf16),
            pltpu.VMEM((last, n_x, pair, feats), bf16),
            pltpu.VMEM((last, n_x, pair, feats), bf16),
            pltpu.VMEM((last, n_x, pair, feats), bf16),
            pltpu.VMEM((last, pair, feats), bf16),
            pltpu.VMEM((last, 2, pair, feats), bf16),
            pltpu.VMEM((2, n_x, ONE, feats), bf16),
            pltpu.VMEM((2, n_x, ONE, feats), bf16),
            pltpu.VMEM((2, n_x, ONE, feats), bf16),
            pltpu.VMEM((2, 3, ONE, feats), bf16),
            pltpu.VMEM((last, pair, feats), bf16),
            pltpu.VMEM((2, ONE, feats), bf16),
            pltpu.VMEM((n_y, capacity, units), bf16),
            pltpu.VMEM((GROUPS, last // GROUPS * pair, units), bf16),
            pltpu.VMEM((2 * ONE, units), bf16),
            pltpu.VMEM((feats, units), jnp.float32),
            dma((n_y - 1,)),
            dma((n_y - 1,)),
            dma((n_y - 1,)),
            dma((n_y - 1,)),
            dma,
            dma((2, half, n_y)),
            dma((2, half, n_y)),
            dma((last + 2,)),
            dma((last + 2,)),
            dma((last, 2)),
            dma((last, 2)),
            dma((last, 2)),
            dma((last, 2)),
            dma((2, 3)),
            dma((2, 3)),
        ],
        compiler_params=pltpu.CompilerParams(
            collective_id=0, has_side_effects=True, vmem_limit_bytes=56 * 1024 * 1024
        ),
        cost_estimate=pl.CostEstimate(
            flops=2 * n_y * capacity * feats * units, bytes_accessed=4 << 20, transcendentals=0
        ),
    )(grad_out, expert_ids.T, slot_ids.T, gate_values.T, hidden[0])
    return result[None]


def solution(mesh):
    in_specs = (
        P(("node", "local", "dp"), None),
        P(("node", "local", "dp"), None),
        P(("node", "local", "dp"), None),
        P(("node", "local", "dp"), None),
        P(("node", "local"), "dp", None),
    )
    out_specs = P(("node", "local"), "dp", None)
    return jax.shard_map(shards, mesh=mesh, in_specs=in_specs, out_specs=out_specs, check_vma=False)
```

```python
import jax
import jax.numpy as jnp
from jax import lax
from jax.experimental import pallas as pl
from jax.experimental.pallas import tpu as pltpu
from jax.sharding import PartitionSpec as P

MESH = pl.DeviceIdType.MESH
LANES = 128
CODE = 8
UNIT = 16
SMALL = 8
GROUP = 4
AHEAD = 3
JUMPS = ((2, AHEAD), (0, 2), (1, 2), (0, 1), (1, 1))


def remote(src, dst, send_sem, recv_sem, **device):
    return pltpu.make_async_remote_copy(
        src_ref=src,
        dst_ref=dst,
        send_sem=send_sem,
        recv_sem=recv_sem,
        device_id=device,
        device_id_type=MESH,
    )


def kernel(
    rows_ref,
    ids_ref,
    slots_ref,
    gates_ref,
    hidden_ref,
    out_ref,
    stage,
    held,
    zbuf,
    near,
    far,
    far_in,
    far_jump,
    far_jump_in,
    near_jump,
    jump_in,
    bucket,
    bucket_jump,
    hid_all,
    hid_perm,
    acc,
    y_send,
    y_recv,
    x_send,
    x_recv,
    h_send,
    h_recv,
    h_local,
    z_send,
    z_recv,
    f_send,
    f_recv,
    d_send,
    d_recv,
    g_send,
    g_recv,
    j_send,
    j_recv,
):
    bf16, f32 = jnp.bfloat16, jnp.float32
    node, z, y = lax.axis_index("node"), lax.axis_index("local"), lax.axis_index("dp")
    n_z, n_y = lax.axis_size("local"), lax.axis_size("dp")
    n_x = lax.axis_size("node") // 2
    x, core = node // 2, lax.rem(node, 2)
    sibling = x * 2 + (1 - core)
    z_up, z_down = lax.rem(z + 1, n_z), lax.rem(z + n_z - 1, n_z)
    n_tok = rows_ref.shape[0]
    half = n_z // 2
    raw = half - AHEAD
    n_unit = raw + 1
    feats = out_ref.shape[0]
    n_col = feats // LANES
    top = ids_ref.shape[0]
    data_rows = n_col * n_tok
    piece = data_rows + top
    lane_group = LANES // n_y
    slots = hidden_ref.shape[0] // n_z
    barrier = pltpu.get_barrier_semaphore()
    greet = [{"dp": lax.rem(y + d, n_y)} for d in range(1, n_y)]
    greet += [{"node": sibling}]
    greet += [
        {"node": lax.rem(x + j, n_x) * 2 + core, "local": lax.rem(z + n_z + step, n_z)}
        for step in (1, -1, 2, -2, AHEAD, -AHEAD)
        for j in range(n_x)
    ]
    greet += [{"node": lax.rem(x + j, n_x) * 2 + core} for j in range(1, n_x)]
    for device in greet:
        pl.semaphore_signal(barrier, inc=1, device_id=device, device_id_type=MESH)

    own_group = lax.rem(x + n_y - y, n_x)

    def on_lanes(values, shift):
        start = lax.rem(own_group + shift, n_x) * lane_group
        put = lax.broadcasted_iota(jnp.int32, (n_tok, LANES), 1) == (
            lax.broadcasted_iota(jnp.int32, (n_tok, LANES), 0) + start
        )
        return jnp.dot(
            values.astype(f32).astype(bf16),
            put.astype(f32).astype(bf16),
            preferred_element_type=f32,
        )

    slot_values = slots_ref[...]
    position = jnp.where(slot_values >= 0, slot_values, CODE - 1)
    routing = on_lanes(ids_ref[...], 0) + on_lanes(position, 1) + on_lanes(gates_ref[...], 2)

    def piece_rows(k):
        return pl.ds(k * piece, piece)

    for d in range(n_y):
        peer = lax.rem(y + d, n_y)
        columns = [
            rows_ref[:, pl.ds(pl.multiple_of(peer * feats + j * LANES, LANES), LANES)].astype(f32)
            for j in range(n_col)
        ]
        whole = jnp.concatenate(columns + [routing], axis=0).astype(bf16)
        if d == 0:
            held[y] = whole
        else:
            stage[d - 1] = whole

    pl.semaphore_wait(barrier, len(greet))

    def y_copy(d):
        return remote(
            stage.at[d - 1],
            held.at[y],
            y_send.at[d - 1],
            y_recv.at[d - 1],
            dp=lax.rem(y + d, n_y),
        )

    def y_arrival(d):
        sender = lax.rem(y + n_y - d, n_y)
        return remote(
            stage.at[d - 1], held.at[sender], y_send.at[d - 1], y_recv.at[d - 1], dp=sender
        )

    def x_copy(replica):
        j = lax.rem(replica + n_x - x, n_x)
        rows = pl.ds(pl.multiple_of((n_x - j) * piece, UNIT), piece)
        return remote(
            held.at[replica],
            zbuf.at[0, 0, rows],
            x_send.at[j - 1],
            x_recv.at[j - 1],
            node=replica * 2 + core,
        )

    def x_arrival(k):
        sender = lax.rem(x + k, n_x)
        return remote(
            held.at[sender],
            zbuf.at[0, 0, piece_rows(k)],
            x_send.at[n_x - 1 - k],
            x_recv.at[n_x - 1 - k],
            node=sender * 2 + core,
        )

    def z_copy(side, slot, to_side, to_slot, k):
        return remote(
            zbuf.at[side, slot, piece_rows(k)],
            zbuf.at[to_side, to_slot, piece_rows(k)],
            z_send.at[side, slot, k],
            z_recv.at[to_side, to_slot, k],
            local=z_up if side == 0 else z_down,
        )

    def z_own(side, k):
        return remote(
            zbuf.at[0, 0, piece_rows(k)],
            zbuf.at[side, 1, piece_rows(k)],
            z_send.at[side, 0, k],
            z_recv.at[side, 1, k],
            local=z_up if side == 0 else z_down,
        )

    def pass_on(replica):
        @pl.when(replica != x)
        def _():
            x_copy(replica).start()

        @pl.when(replica == x)
        def _():
            zbuf[0, 0, :piece, :] = held[replica]
            for side in range(2):
                z_own(side, 0).start()

    for d in (1, n_y - 1, 2):
        y_copy(d).start()
    pass_on(y)
    for d in (1, n_y - 1, 2):
        y_arrival(d).wait_recv()
        pass_on(lax.rem(y + n_y - d, n_y))
    x_arrival(1).wait_recv()
    z_own(0, 1).start()
    x_arrival(3).wait_recv()
    z_own(1, 3).start()
    z_own(0, 3).start()
    x_arrival(2).wait_recv()
    z_own(1, 2).start()
    z_own(0, 2).start()
    z_own(1, 1).start()
    order = ((0, 1, 3, 2), (0, 3, 2, 1))

    def h_copy(d):
        return remote(
            hidden_ref,
            hid_all.at[y],
            h_send.at[d - 1],
            h_recv.at[d - 1],
            dp=lax.rem(y + d, n_y),
        )

    def h_arrival(d):
        sender = lax.rem(y + n_y - d, n_y)
        return remote(
            hidden_ref, hid_all.at[sender], h_send.at[d - 1], h_recv.at[d - 1], dp=sender
        )

    for d in range(1, n_y):
        h_copy(d).start()
    own_hidden = pltpu.make_async_copy(hidden_ref, hid_all.at[y], h_local)
    own_hidden.start()

    def far_copy(b):
        return remote(far.at[b], far_in.at[b], f_send.at[b], f_recv.at[b], node=sibling)

    def direct_copy(b, j):
        chip = lax.rem(x + j, n_x)
        return remote(
            near.at[b, chip],
            bucket.at[b, x],
            d_send.at[b, j - 1],
            d_recv.at[b, j - 1],
            node=chip * 2 + core,
        )

    def direct_arrival(b, j):
        sender = lax.rem(x + n_x - j, n_x)
        return remote(
            near.at[b, sender],
            bucket.at[b, sender],
            d_send.at[b, j - 1],
            d_recv.at[b, j - 1],
            node=sender * 2 + core,
        )

    chip_of = lax.broadcasted_iota(jnp.int32, (n_x, UNIT, LANES), 0)
    row_of = lax.broadcasted_iota(jnp.int32, (n_x, UNIT, LANES), 1)
    lane_of = lax.broadcasted_iota(jnp.int32, (top, LANES), 1) // lane_group

    def read_block(side, slot):
        block = zbuf[side, slot].astype(f32)
        gap = jnp.zeros((lane_group - n_tok, LANES), f32)
        columns = []
        for j in range(n_col):
            rows = []
            for k in range(n_y):
                start = k * piece + j * n_tok
                rows += [block[start : start + n_tok], gap]
            columns.append(jnp.concatenate(rows, axis=0))
        values = jnp.concatenate(columns, axis=1).astype(bf16)
        parts = []
        for shift in range(3):
            part = jnp.zeros((top, LANES), f32)
            for k in range(n_y):
                held = block[k * piece + data_rows : (k + 1) * piece]
                part = jnp.where(lane_of == (k + shift) % n_y, held, part)
            parts.append(
                pltpu.roll(part, LANES - shift * lane_group, 1) if shift else part
            )
        return values, parts[0] * float(CODE) + parts[1], parts[2]

    def weights(side, codes, gates, which):
        code = ((chip_of * 2 + which) * n_z + z) * CODE + row_of - side * slots
        mine = (row_of >= side * slots) & (row_of < (side + 1) * slots)
        target = jnp.where(mine, code, -1).astype(f32)
        weight = jnp.zeros((n_x, UNIT, LANES), f32)
        for k in range(top):
            weight = weight + jnp.where(
                codes[k : k + 1, :][None] == target, gates[k : k + 1, :][None], 0.0
            )
        return weight.reshape(n_x * UNIT, LANES)

    def place(slot, b, sides):
        blocks = [read_block(side, slot) for side in sides]
        values = jnp.concatenate([values for values, _, _ in blocks], axis=0)
        rows = [
            jnp.concatenate([weights(side, *blocks[side][1:], which) for side in sides], axis=1)
            for which in (1 - core, core)
        ]
        placed = jnp.dot(
            jnp.concatenate(rows, axis=0).astype(bf16), values, preferred_element_type=f32
        ).astype(bf16)
        far[b] = placed[: n_x * UNIT].reshape(n_x, UNIT, feats)
        far_copy(b).start()
        near[b] = placed[n_x * UNIT :].reshape(n_x, UNIT, feats)

    def jump_place(side, step, which):
        if side == 2:
            return lax.rem(z + n_z + jnp.where(which == 0, step, -step), n_z)
        return lax.rem(z + n_z + (step if side == 0 else -step), n_z)

    small_chip = lax.broadcasted_iota(jnp.int32, (n_x, SMALL, LANES), 0)
    small_row = lax.broadcasted_iota(jnp.int32, (n_x, SMALL, LANES), 1)

    def jump_weights(side, codes, gates, which):
        parts = []
        for way, step in JUMPS:
            weight = jnp.zeros((n_x, SMALL, LANES), f32)
            if way in (side, 2):
                code = ((small_chip * 2 + which) * n_z + jump_place(way, step, which)) * CODE
                mine = small_row < slots
                if way == 2:
                    mine = mine & (which == side)
                target = jnp.where(mine, code + small_row, -1).astype(f32)
                for k in range(top):
                    weight = weight + jnp.where(
                        codes[k : k + 1, :][None] == target, gates[k : k + 1, :][None], 0.0
                    )
            parts.append(weight.reshape(n_x * SMALL, LANES))
        return jnp.concatenate(parts, axis=0)

    def place_jumps():
        blocks = [read_block(side, raw) for side in range(2)]
        values = jnp.concatenate([values for values, _, _ in blocks], axis=0)
        gap = jnp.zeros((near_jump.shape[2] - n_col * SMALL, LANES), f32)
        for which, dest in ((1 - core, far_jump), (core, near_jump)):
            rows = [jump_weights(side, *blocks[side][1:], which) for side in range(2)]
            placed = jnp.dot(
                jnp.concatenate(rows, axis=1).astype(bf16), values, preferred_element_type=f32
            )
            for g in range(len(JUMPS)):
                for chip in range(n_x):
                    start = (g * n_x + chip) * SMALL
                    part = placed[start : start + SMALL]
                    columns = [part[:, j * LANES : (j + 1) * LANES] for j in range(n_col)]
                    dest[g, chip] = jnp.concatenate(columns + [gap], axis=0).astype(bf16)
                if dest is far_jump:
                    far_jump_copy(g).start()

    def far_jump_copy(g):
        return remote(
            far_jump.at[g], far_jump_in.at[g], g_send.at[g], g_recv.at[g], node=sibling
        )

    def jump_copy(g, j):
        chip = lax.rem(x + j, n_x)
        return remote(
            near_jump.at[g, chip],
            jump_in.at[g, x],
            j_send.at[g, j],
            j_recv.at[g, j],
            node=chip * 2 + core,
            local=jump_place(*JUMPS[g], core),
        )

    def jump_arrival(g, j):
        sender = lax.rem(x + n_x - j, n_x)
        way, step = JUMPS[g]
        return remote(
            near_jump.at[g, sender],
            jump_in.at[g, sender],
            j_send.at[g, j],
            j_recv.at[g, j],
            node=sender * 2 + core,
            local=jump_place(way, -step, core),
        )

    def merge_jumps():
        for g in range(len(JUMPS)):
            far_jump_copy(g).wait_recv()
            near_jump[g] = near_jump[g] + far_jump_in[g]
            for j in (2, 1, 3, 0):
                jump_copy(g, j).start()

    def finish_jumps():
        for g in (3, 4, 1, 2, 0):
            rows = []
            for j in range(n_x):
                jump_arrival(g, j).wait_recv()
            for replica in range(n_y):
                part = jump_in[g, replica].astype(f32)
                rows.append(
                    jnp.concatenate(
                        [part[j * SMALL : (j + 1) * SMALL] for j in range(n_col)], axis=1
                    )
                )
            count = n_y * SMALL
            bucket_jump[g * count : (g + 1) * count, :] = jnp.concatenate(rows, axis=0).astype(bf16)

    def merge(b):
        far_copy(b).wait_recv()
        near[b] = near[b] + far_in[b]
        for j in (2, 1, 3):
            direct_copy(b, j).start()
        bucket[b, x] = near[b, x]

    def finish(b):
        for j in range(1, n_x):
            direct_arrival(b, j).wait_recv()

    positions = n_y * n_z * slots
    group = GROUP * n_y * UNIT

    def choose(column, start):
        count = column.shape[0]
        pick = lax.broadcasted_iota(jnp.int32, (count, positions), 1) == column
        hid_perm[pl.ds(start, count), :] = jnp.dot(
            pick.astype(bf16),
            hid_all[...].reshape(positions, hid_all.shape[2]),
            preferred_element_type=f32,
        ).astype(bf16)

    def unit_columns(count, first):
        i = lax.broadcasted_iota(jnp.int32, (count, 1), 0)
        unit = lax.div(i, n_y * UNIT) + first
        replica = lax.rem(lax.div(i, UNIT), n_y)
        at = lax.rem(i, UNIT)
        above = at >= slots
        step = jnp.where(unit < raw, unit + 1, 0)
        source = lax.rem(jnp.where(above, z + step, z - step + n_z), n_z)
        column = replica * (n_z * slots) + source * slots + jnp.where(above, at - slots, at)
        used = jnp.where(unit < raw, 2 * slots, slots)
        return jnp.where(at < used, column, -1)

    def order_hidden(g):
        choose(unit_columns(group, g * GROUP), pl.multiple_of(g * group, UNIT))

    def order_hidden_rest():
        full = raw // GROUP * GROUP
        choose(unit_columns((n_unit - full) * n_y * UNIT, full), full * n_y * UNIT)
        parts = []
        for way, step in JUMPS:
            i = lax.broadcasted_iota(jnp.int32, (n_y * SMALL, 1), 0)
            replica, at = lax.div(i, SMALL), lax.rem(i, SMALL)
            far_off = raw + step
            source = lax.rem(z + far_off if way == 1 else z + n_z - far_off, n_z)
            column = replica * (n_z * slots) + source * slots + at
            parts.append(jnp.where(at < slots, column, -1))
        choose(jnp.concatenate(parts, axis=0), n_unit * n_y * UNIT)

    def product(low, high, j):
        cols = pl.ds(pl.multiple_of(j * LANES, LANES), LANES)
        start, stop = low * n_y * UNIT, high * n_y * UNIT
        if low == n_unit:
            stop = hid_perm.shape[0]
            left = bucket_jump[:, cols]
        else:
            left = bucket[low:high, :, :, cols].reshape(stop - start, LANES)
        term = lax.dot_general(
            left,
            hid_perm[start:stop, :],
            (((0,), (0,)), ((), ())),
            preferred_element_type=f32,
        )
        if low > 0:
            term = term + acc[cols, :]
        if low < n_unit:
            acc[cols, :] = term
        else:
            out_ref[cols, :] = term.astype(bf16)

    def products(low, high):
        @pl.loop(0, n_col)
        def _(j):
            product(low, high, j)

    hidden_at = 6
    first_at = hidden_at + 2
    second_at = first_at + (n_col + 1) // 2
    place(0, raw, (0,))

    @pl.loop(1, raw + 1)
    def _(t):
        def z_step(at):
            for side in range(2):
                k = order[side][at]
                z_copy(side, t - 1, side, t, k).wait_recv()

                @pl.when(t < raw)
                def _():
                    z_copy(side, t, side, t + 1, k).start()

        z_step(0)
        z_step(1)

        @pl.when(t > 1)
        def _():
            merge(t - 2)

        @pl.when(t == 1)
        def _():
            merge(raw)

        z_step(2)

        @pl.when(t == hidden_at)
        def _():
            for d in range(1, n_y):
                h_arrival(d).wait_recv()
            own_hidden.wait()

        @pl.when((t > hidden_at) & (t <= hidden_at + raw // GROUP))
        def _():
            order_hidden(t - hidden_at - 1)

        @pl.when(t == hidden_at + raw // GROUP + 1)
        def _():
            order_hidden_rest()

        @pl.when((t >= first_at) & (t < second_at))
        def _():
            j = (t - first_at) * 2
            product(0, GROUP, j)

            @pl.when(j + 1 < n_col)
            def _():
                product(0, GROUP, j + 1)

        @pl.when(t >= second_at)
        def _():
            j = (t - second_at) * 2
            product(GROUP, 2 * GROUP, j)
            product(GROUP, 2 * GROUP, j + 1)

        z_step(3)

        @pl.when(t == raw)
        def _():
            place_jumps()

        place(t, t - 1, (0, 1))

        @pl.when(t > 2)
        def _():
            finish(t - 3)

    merge_jumps()
    merge(raw - 1)
    finish(raw)
    for j in range(2 * (raw + 1 - second_at), n_col):
        product(GROUP, 2 * GROUP, j)
    finish(raw - 2)
    products(2 * GROUP, 3 * GROUP)
    finish(raw - 1)
    products(3 * GROUP, n_unit)
    finish_jumps()
    products(n_unit, n_unit + 1)

    for d in range(1, n_y):
        y_copy(d).wait_send()
        h_copy(d).wait_send()
    for k in range(n_y):
        for side in range(2):
            z_own(side, k).wait_send()

            @pl.loop(1, raw)
            def _(t):
                z_copy(side, t, side, t + 1, k).wait_send()

    for j in range(1, n_x):
        x_copy(lax.rem(x + j, n_x)).wait_send()

    @pl.loop(0, n_unit)
    def _(b):
        far_copy(b).wait_send()
        for j in range(1, n_x):
            direct_copy(b, j).wait_send()

    for g in range(len(JUMPS)):
        far_jump_copy(g).wait_send()
        for j in range(n_x):
            jump_copy(g, j).wait_send()


def shards(grad_out, expert_ids, slot_ids, gate_values, hidden):
    n_x = lax.axis_size("node") // 2
    n_z, n_y = lax.axis_size("local"), lax.axis_size("dp")
    n_tok, width = grad_out.shape
    top = expert_ids.shape[1]
    _, capacity, units = hidden.shape
    feats = width // n_y
    raw = n_z // 2 - AHEAD
    n_unit = raw + 1
    jump_rows = pl.cdiv(feats // LANES * SMALL, UNIT) * UNIT
    piece = feats // LANES * n_tok + top
    bf16 = jnp.bfloat16
    vmem = pl.BlockSpec(memory_space=pltpu.VMEM)
    dma = pltpu.SemaphoreType.DMA
    result = pl.pallas_call(
        kernel,
        out_shape=pltpu.VMEM((feats, units), bf16),
        in_specs=[vmem] * 4 + [pl.BlockSpec(memory_space=pl.ANY)],
        out_specs=vmem,
        scratch_shapes=[
            pltpu.VMEM((n_y - 1, piece, LANES), bf16),
            pltpu.VMEM((n_y, piece, LANES), bf16),
            pltpu.VMEM((2, raw + 1, n_y * piece, LANES), bf16),
            pltpu.VMEM((n_unit, n_x, UNIT, feats), bf16),
            pltpu.VMEM((n_unit, n_x, UNIT, feats), bf16),
            pltpu.VMEM((n_unit, n_x, UNIT, feats), bf16),
            pltpu.VMEM((len(JUMPS), n_x, jump_rows, LANES), bf16),
            pltpu.VMEM((len(JUMPS), n_x, jump_rows, LANES), bf16),
            pltpu.VMEM((len(JUMPS), n_x, jump_rows, LANES), bf16),
            pltpu.VMEM((len(JUMPS), n_x, jump_rows, LANES), bf16),
            pltpu.VMEM((n_unit, n_y, UNIT, feats), bf16),
            pltpu.VMEM((len(JUMPS) * n_y * SMALL, feats), bf16),
            pltpu.VMEM((n_y, capacity, units), bf16),
            pltpu.VMEM((n_unit * n_y * UNIT + len(JUMPS) * n_y * SMALL, units), bf16),
            pltpu.VMEM((feats, units), jnp.float32),
            dma((n_y - 1,)),
            dma((n_y - 1,)),
            dma((n_x - 1,)),
            dma((n_x - 1,)),
            dma((n_y - 1,)),
            dma((n_y - 1,)),
            dma,
            dma((2, raw + 1, n_y)),
            dma((2, raw + 1, n_y)),
            dma((n_unit,)),
            dma((n_unit,)),
            dma((n_unit, n_x - 1)),
            dma((n_unit, n_x - 1)),
            dma((len(JUMPS),)),
            dma((len(JUMPS),)),
            dma((len(JUMPS), n_x)),
            dma((len(JUMPS), n_x)),
        ],
        compiler_params=pltpu.CompilerParams(
            collective_id=0, has_side_effects=True, vmem_limit_bytes=56 * 1024 * 1024
        ),
        cost_estimate=pl.CostEstimate(
            flops=2 * n_y * capacity * feats * units, bytes_accessed=4 << 20, transcendentals=0
        ),
    )(grad_out, expert_ids.T, slot_ids.T, gate_values.T, hidden[0])
    return result[None]


def solution(mesh):
    in_specs = (
        P(("node", "local", "dp"), None),
        P(("node", "local", "dp"), None),
        P(("node", "local", "dp"), None),
        P(("node", "local", "dp"), None),
        P(("node", "local"), "dp", None),
    )
    out_specs = P(("node", "local"), "dp", None)
    return jax.shard_map(shards, mesh=mesh, in_specs=in_specs, out_specs=out_specs, check_vma=False)
```
